256 devices in a mesh: outer: 16 (over y_lo, z), inner: 16 (over x, y_hi, core).
Axes of the slice: x: 4, y: 4 (y_hi: 2, y_lo: 2; y = y_hi * 2 + y_lo), z: 8, core: 2. Of those that a mesh axis runs over, the one named last changes fastest.
Arguments:
- queries: bfloat16 [65536, 8, 256], P(('outer', 'inner')), may hold values from -6 to 6
- key_heads: bfloat16 [65536, 4, 256], P(('outer', 'inner')), may hold values from -6 to 6
- value_heads: bfloat16 [65536, 4, 256], P(('outer', 'inner')), may hold values from -6 to 6
- grad_output: bfloat16 [65536, 8, 256], P(('outer', 'inner')), may hold values from -6 to 6
- documents: int32 [65536], P(('outer', 'inner')), may hold values from 0 to 127, never falling along the last dimension, each value on 1 to 1024 neighbouring positions
Outputs:
- attended: bfloat16 [65536, 8, 256], P(('outer', 'inner'))
- grad_queries: bfloat16 [65536, 8, 256], P(('outer', 'inner'))
- grad_keys: bfloat16 [65536, 4, 256], P(('outer', 'inner'))
- grad_values: bfloat16 [65536, 4, 256], P(('outer', 'inner'))
The draws below stay inside these ranges and needn't reach their ends.
Inputs may be any that keep to these rules, and one draw needn't show every extreme that they name: `documents`: document ids never fall along the sequence; each document has 1 to 1024 tokens and one has exactly 1024.
All inputs are finite; a program needn't handle non-finite values.
Results may differ from the reference program's by a relative error of at most 0.019.
Values may be sent and summed in bfloat16 or wider, within the bound.
No kernel may reach another device: no remote copies, remote signals or barrier semaphores. Data moves between devices by JAX's collectives and lax.ppermute only.
A program may use at most 64 MiB of HBM per device.

```python
import math
import jax
import jax.numpy as jnp
import numpy as np
from jax import lax

H = 8
KVH = 4
HD = 256
TOK_DEV = 256
TOKENS = 65536
WINDOW = 512
DOCS = 128
MAX_DOC = 1024


def shared_direction(key):
    signed = jax.random.bernoulli(jax.random.fold_in(key, 101), 0.5, (KVH, HD))
    return jnp.where(signed, 1.0, -1.0).astype(jnp.float32)


def draw_queries(key, part):
    direction = shared_direction(key)
    key = jax.random.fold_in(key, 1)
    key_jitter, key_chosen, key_height, key_modest = jax.random.split(key, 4)
    jitter = jax.random.truncated_normal(key_jitter, -3.0, 3.0, (TOKENS, H, HD), jnp.float32)
    chosen = jax.random.bernoulli(key_chosen, 0.25, (TOKENS, H, 1))
    height = jax.random.uniform(key_height, (TOKENS, H, 1), jnp.float32, 1.0, 2.5)
    modest = jax.random.uniform(key_modest, (TOKENS, H, 1), jnp.float32, 0.0, 0.3)
    factor = jnp.where(chosen, height, modest)
    per_head = jnp.repeat(direction, H // KVH, axis=0)
    return (jitter + factor * per_head[None, :, :]).astype(jnp.bfloat16)


def draw_key_heads(key, part):
    direction = shared_direction(key)
    key = jax.random.fold_in(key, 2)
    key_jitter, key_factor = jax.random.split(key, 2)
    jitter = jax.random.truncated_normal(key_jitter, -3.0, 3.0, (TOKENS, KVH, HD), jnp.float32)
    factor = jax.random.uniform(key_factor, (TOKENS, KVH, 1), jnp.float32, -1.5, 1.5)
    return (jitter + factor * direction[None, :, :]).astype(jnp.bfloat16)


def steps_of(stream_key, shape, shards, least, top_value):
    level, own = 1.0, jax.random.fold_in(stream_key, 6)
    for axis_at, blocks in shards:
        draws = jnp.exp(jax.random.uniform(jax.random.fold_in(own, axis_at), (blocks,), jnp.float32, least / len(shards), top_value / len(shards)))
        level = level * jnp.repeat(draws, shape[axis_at] // blocks).reshape([-1 if axis == axis_at else 1 for axis in range(len(shape))])
    return level


def length_profile(count, total, limit, lean):
    loads = [(1 << 20) // math.isqrt(standing ** lean) + 1 for standing in range(2, count + 1)]
    surplus, holding = total - limit - (count - 1), [1] * (count - 1)
    while surplus > 0:
        movable = [i for i in range(count - 1) if holding[i] < limit]
        mass, left = sum([loads[i] for i in movable]), surplus
        for i in movable:
            more = min(limit - holding[i], max(1, left * loads[i] // mass), surplus)
            holding[i] = holding[i] + more
            surplus = surplus - more
    return np.array([limit] + holding)


def ragged_sizes(stream_key, number_of, total, reach, skew):
    if number_of == 2:
        one = jax.random.randint(stream_key, (), max(1, total - reach), min(reach, total - 1) + 1)
        return jnp.stack([one, total - one])
    sizes = jnp.asarray(length_profile(number_of, total, reach, skew), jnp.int32)
    couples = (number_of - 1) // 2
    source_of, sink = sizes[1:1 + 2 * couples:2], sizes[2:2 + 2 * couples:2]
    slack = jnp.minimum(source_of - 1, reach - sink)
    passed = jax.random.randint(jax.random.fold_in(stream_key, 1), (couples,), 0, 1 << 20) % (slack + 1)
    sizes = sizes.at[1:1 + 2 * couples:2].set(source_of - passed).at[2:2 + 2 * couples:2].set(sink + passed)
    return sizes[jax.random.permutation(jax.random.fold_in(stream_key, 2), number_of)]


def normal_values(rng, dims, width, bound, cuts=(), held_as=jnp.bfloat16):
    loudness = steps_of(rng, dims, cuts, -0.22, 0.18) if cuts else 1.0
    array = jax.random.normal(rng, dims, jnp.float32) * width * loudness
    return jnp.minimum(jnp.maximum(array, -bound), bound).astype(held_as)


def setup_inputs(seed: int = 0) -> dict:
    splits = jax.random.split(jax.random.key(seed), 6)
    return {
        "queries": draw_queries(jax.random.fold_in(splits[5], 71), 0),
        "key_heads": draw_key_heads(jax.random.fold_in(splits[5], 71), 0),
        "value_heads": normal_values(splits[2], (TOKENS, KVH, HD), 1.0, 6.0, ((0, 256),)),
        "grad_output": normal_values(splits[3], (TOKENS, H, HD), 1.0, 6.0, ((0, 256),)),
        "documents": jnp.searchsorted(jnp.cumsum(ragged_sizes(splits[4], DOCS, TOKENS, MAX_DOC, 1)), jnp.arange(TOKENS), side="right").astype(jnp.int32),
    }


SOFTCAP = 50.0


def attend(queries, key_rows, value_rows, grad_out, doc_query, doc_key, query_pos, key_pos, window):
    row_count, heads, head_size = queries.shape
    kv_heads = key_rows.shape[1]
    groups = heads // kv_heads
    score_scale = head_size ** -0.5
    grouped = queries.reshape(row_count, kv_heads, groups, head_size).astype(jnp.float32)
    keys_wide = key_rows.astype(jnp.float32)
    values_wide = value_rows.astype(jnp.float32)
    scores = jnp.einsum('tkgd,skd->kgts', grouped, keys_wide) * score_scale
    capped = SOFTCAP * jnp.tanh(scores / SOFTCAP)
    distance = query_pos[:, None] - key_pos[None, :]
    allowed = (doc_query[:, None] == doc_key[None, :]) & (distance >= 0) & (distance < window) & (key_pos[None, :] >= 0)
    raised = jnp.where(allowed, jnp.exp(capped), jnp.float32(0.0))
    probs = raised / jnp.sum(raised, axis=-1, keepdims=True)
    probs_half = probs.astype(jnp.bfloat16).astype(jnp.float32)
    output = jnp.einsum('kgts,skd->tkgd', probs_half, values_wide).astype(jnp.bfloat16)
    upstream = grad_out.reshape(row_count, kv_heads, groups, head_size).astype(jnp.float32)
    row_delta = jnp.einsum('tkgd,tkgd->kgt', upstream, output.astype(jnp.float32))
    grad_probs = jnp.einsum('tkgd,skd->kgts', upstream, values_wide)
    grad_scores = (probs * (grad_probs - row_delta[..., None]) * (1.0 - (capped / SOFTCAP) ** 2)).astype(jnp.bfloat16).astype(jnp.float32)
    grad_query = (jnp.einsum('kgts,skd->tkgd', grad_scores, keys_wide) * score_scale).astype(jnp.bfloat16)
    grad_key = jnp.einsum('kgts,tkgd->skd', grad_scores, grouped) * score_scale
    grad_value = jnp.einsum('kgts,tkgd->skd', probs_half, upstream)
    return (output.reshape(row_count, heads, head_size), grad_query.reshape(row_count, heads, head_size), grad_key, grad_value)


def reference(queries, key_heads, value_heads, grad_output, documents):
    blocks = TOKENS // TOK_DEV
    query_blocks = queries.reshape(blocks, TOK_DEV, H, HD)
    grad_blocks = grad_output.reshape(blocks, TOK_DEV, H, HD)
    key_padded = jnp.concatenate([jnp.zeros((2 * TOK_DEV, KVH, HD), jnp.bfloat16), key_heads], axis=0)
    value_padded = jnp.concatenate([jnp.zeros((2 * TOK_DEV, KVH, HD), jnp.bfloat16), value_heads], axis=0)
    doc_padded = jnp.concatenate([jnp.zeros((2 * TOK_DEV,), jnp.int32), documents.astype(jnp.int32)], axis=0)

    def one_block(block_index):
        first_token = (block_index * TOK_DEV).astype(jnp.int32)
        key_rows = lax.dynamic_slice_in_dim(key_padded, first_token, 3 * TOK_DEV, 0)
        value_rows = lax.dynamic_slice_in_dim(value_padded, first_token, 3 * TOK_DEV, 0)
        doc_key = lax.dynamic_slice_in_dim(doc_padded, first_token, 3 * TOK_DEV, 0)
        doc_query = lax.dynamic_slice_in_dim(doc_padded, first_token + 2 * TOK_DEV, TOK_DEV, 0)
        query_pos = first_token + jnp.arange(TOK_DEV, dtype=jnp.int32)
        key_pos = first_token - 2 * TOK_DEV + jnp.arange(3 * TOK_DEV, dtype=jnp.int32)
        block_queries = lax.dynamic_index_in_dim(query_blocks, block_index, 0, keepdims=False)
        block_grads = lax.dynamic_index_in_dim(grad_blocks, block_index, 0, keepdims=False)
        output, grad_query, grad_key, grad_value = attend(block_queries, key_rows, value_rows, block_grads, doc_query, doc_key, query_pos, key_pos, WINDOW)
        return (output, grad_query, grad_key[2 * TOK_DEV:], grad_value[2 * TOK_DEV:],
                grad_key[TOK_DEV:2 * TOK_DEV].astype(jnp.bfloat16), grad_value[TOK_DEV:2 * TOK_DEV].astype(jnp.bfloat16),
                grad_key[:TOK_DEV].astype(jnp.bfloat16), grad_value[:TOK_DEV].astype(jnp.bfloat16))

    results = lax.map(one_block, jnp.arange(blocks, dtype=jnp.int32))
    output, grad_query, own_key, own_value, near_key, near_value, far_key, far_value = results
    near_key, near_value, far_key, far_value = lax.optimization_barrier((near_key, near_value, far_key, far_value))
    empty_one = jnp.zeros((1, TOK_DEV, KVH, HD), jnp.bfloat16)
    empty_two = jnp.zeros((2, TOK_DEV, KVH, HD), jnp.bfloat16)
    near_key = jnp.concatenate([near_key[1:], empty_one], axis=0)
    near_value = jnp.concatenate([near_value[1:], empty_one], axis=0)
    far_key = jnp.concatenate([far_key[2:], empty_two], axis=0)
    far_value = jnp.concatenate([far_value[2:], empty_two], axis=0)
    grad_keys = (own_key + near_key.astype(jnp.float32) + far_key.astype(jnp.float32)).astype(jnp.bfloat16)
    grad_values = (own_value + near_value.astype(jnp.float32) + far_value.astype(jnp.float32)).astype(jnp.bfloat16)
    return (output.reshape(TOKENS, H, HD), grad_query.reshape(TOKENS, H, HD),
            grad_keys.reshape(TOKENS, KVH, HD), grad_values.reshape(TOKENS, KVH, HD))
```

```python
import functools

import jax
import jax.numpy as jnp
from jax import lax
from jax.experimental import pallas as pl
from jax.experimental.pallas import tpu as pltpu
from jax.sharding import PartitionSpec as P

SOFTCAP = 50.0
AXES = ("outer", "inner")
ANY = pl.BlockSpec(memory_space=pl.ANY)
VMEM = pl.BlockSpec(memory_space=pltpu.VMEM)
SMEM = pl.BlockSpec(memory_space=pltpu.SMEM)
HBM = pl.BlockSpec(memory_space=pltpu.HBM)
PIECES = 4
DOC_ROWS = 16
CHEAP = pl.CostEstimate(flops=1000, bytes_accessed=1000, transcendentals=0)
SOME = pl.CostEstimate(flops=10**11, bytes_accessed=1 << 30, transcendentals=0)


def times_transposed(a, b):
    return lax.dot_general(a, b, (((1,), (1,)), ((), ())), preferred_element_type=jnp.float32)


def times(a, b):
    return jnp.dot(a, b, preferred_element_type=jnp.float32)


def pieces(block):
    step = block // PIECES
    return [slice(n * step, (n + 1) * step) for n in range(PIECES)]


def fetch(sources, targets, sems):
    copies = []
    for n, at in enumerate(pieces(sources[0].shape[0])):
        for m, (source, target) in enumerate(zip(sources, targets)):
            span = pl.ds(at.start, at.stop - at.start)
            copies.append(pltpu.make_async_copy(source.at[span], target.at[span], sems.at[n, m]))
    for copy in copies:
        copy.start()
    return copies


def split_kernel(core_ref, keys, values, documents, *rest):
    outs, (key_buf, value_buf, doc_buf, sems) = rest[:4], rest[4:]
    block = keys.shape[0]
    copies = fetch((keys, values), (key_buf, value_buf), sems)
    doc_copy = pltpu.make_async_copy(documents, doc_buf, sems.at[PIECES, 0])
    doc_copy.start()

    def place(first):
        for n, at in enumerate(pieces(block)):
            copies[2 * n].wait()
            copies[2 * n + 1].wait()
            for r, out in enumerate(outs):
                head = (first + r) % 4
                out[at, :] = key_buf[at, head, :]
                out[block + at.start : block + at.stop, :] = value_buf[at, head, :]

    @pl.when(core_ref[0] == 0)
    def _():
        place(0)

    @pl.when(core_ref[0] == 1)
    def _():
        place(2)

    doc_copy.wait()
    line = (doc_buf[...] + 1).astype(jnp.float32)
    ids = jnp.broadcast_to(line, (DOC_ROWS, block)).astype(jnp.bfloat16)
    for out in outs:
        out[2 * block :, :] = ids


def split(core, keys, values, documents):
    block, heads, size = keys.shape
    shape = jax.ShapeDtypeStruct((2 * block + DOC_ROWS, size), jnp.bfloat16)
    return pl.pallas_call(
        split_kernel,
        out_shape=(shape,) * heads,
        in_specs=[SMEM, HBM, HBM, HBM],
        out_specs=(VMEM,) * heads,
        scratch_shapes=[
            pltpu.VMEM(keys.shape, jnp.bfloat16),
            pltpu.VMEM(values.shape, jnp.bfloat16),
            pltpu.VMEM(documents.shape, jnp.int32),
            pltpu.SemaphoreType.DMA((PIECES + 1, 2)),
        ],
        compiler_params=pltpu.CompilerParams(vmem_limit_bytes=60 << 20),
        cost_estimate=CHEAP,
    )(core, keys, values, documents)


def arrange_kernel(core_ref, queries, upstream, *refs):
    kv, outs = refs[:4], refs[4:]
    rows = 2 * queries.shape[0]
    size = queries.shape[2]
    for r, source in enumerate(kv):
        outs[r // 2][r % 2, 2 * rows :, :] = source[...]

    def place(core):
        for r in range(4):
            head = (2 * core + r) % 4
            for n, x in enumerate((queries, upstream)):
                part = x[:, 2 * head : 2 * head + 2, :].reshape(rows, size)
                outs[r // 2][r % 2, n * rows : (n + 1) * rows, :] = part

    by_core(core_ref, place)


def arrange(core, queries, upstream, kv):
    block, heads, size = queries.shape
    shape = jax.ShapeDtypeStruct((2, 4 * block + kv[0].shape[0], size), jnp.bfloat16)
    return pl.pallas_call(
        arrange_kernel,
        out_shape=(shape, shape),
        in_specs=[SMEM] + [VMEM] * 6,
        out_specs=(VMEM, VMEM),
        compiler_params=pltpu.CompilerParams(vmem_limit_bytes=20 << 20),
        cost_estimate=CHEAP,
    )(core, queries, upstream, *kv)


def hold_kernel(core_ref, *refs):
    refs[-1][0] = core_ref[0]


def hold(core, *values):
    return pl.pallas_call(
        hold_kernel,
        out_shape=jax.ShapeDtypeStruct((1,), jnp.int32),
        in_specs=[SMEM] + [VMEM] * len(values),
        out_specs=SMEM,
        compiler_params=pltpu.CompilerParams(vmem_limit_bytes=8 << 20),
        cost_estimate=SOME,
    )(core, *values)


def spread_kernel(core_ref, after, own_0, own_1, other_0, other_1, attended, grad_queries, done):
    block, _, size = attended.shape
    rows = 2 * block
    done[0] = core_ref[0]

    def place(core):
        order = (own_0, own_1, other_0, other_1) if core == 0 else (other_0, other_1, own_0, own_1)
        for g, part in enumerate(order):
            for n, out in enumerate((attended, grad_queries)):
                out[:, 2 * g : 2 * g + 2, :] = part[n * rows : (n + 1) * rows, :].reshape(
                    block, 2, size
                )

    by_core(core_ref, place)


def spread(core, after, block, own, other):
    size = own[0].shape[1]
    shape = jax.ShapeDtypeStruct((block, 8, size), jnp.bfloat16)
    return pl.pallas_call(
        spread_kernel,
        out_shape=(shape, shape, jax.ShapeDtypeStruct((1,), jnp.int32)),
        in_specs=[SMEM, SMEM] + [VMEM] * 4,
        out_specs=(VMEM, VMEM, SMEM),
        compiler_params=pltpu.CompilerParams(vmem_limit_bytes=20 << 20),
        cost_estimate=CHEAP,
    )(core, after, *own, *other)


def gather_kernel(core_ref, *refs):
    own, other, same, cross = refs[:2], refs[2:4], refs[4:6], refs[6:8]
    outs, bufs, sems = refs[9:11], refs[11:13], refs[13]
    block = outs[0].shape[0]
    base = own[0].shape[0] - 2 * block
    near, far = list(zip(own, same)), list(zip(other, cross))

    def place(order):
        for p, at in enumerate(pieces(block)):
            for n in range(2):
                for g, (here, there) in enumerate(order):
                    first = n * block + at.start
                    last = n * block + at.stop
                    a = here[base + first : base + last, :].astype(jnp.float32)
                    b = there[first:last, :].astype(jnp.float32)
                    bufs[n][at, g, :] = (a + b).astype(jnp.bfloat16)
                span = pl.ds(at.start, at.stop - at.start)
                pltpu.make_async_copy(bufs[n].at[span], outs[n].at[span], sems.at[p, n]).start()

    @pl.when(core_ref[0] == 0)
    def _():
        place(near + far)

    @pl.when(core_ref[0] == 1)
    def _():
        place(far + near)

    for p, at in enumerate(pieces(block)):
        span = pl.ds(at.start, at.stop - at.start)
        for n in range(2):
            pltpu.make_async_copy(bufs[n].at[span], outs[n].at[span], sems.at[p, n]).wait()


def gather(core, block, own, other, same, cross, after):
    size = own[0].shape[1]
    shape = jax.ShapeDtypeStruct((block, 4, size), jnp.bfloat16)
    return pl.pallas_call(
        gather_kernel,
        out_shape=(shape, shape),
        in_specs=[SMEM] + [VMEM] * 8 + [SMEM],
        out_specs=(HBM, HBM),
        scratch_shapes=[
            pltpu.VMEM((block, 4, size), jnp.bfloat16),
            pltpu.VMEM((block, 4, size), jnp.bfloat16),
            pltpu.SemaphoreType.DMA((PIECES, 2)),
        ],
        compiler_params=pltpu.CompilerParams(vmem_limit_bytes=20 << 20),
        cost_estimate=CHEAP,
    )(core, *own, *other, *same, *cross, after)


def by_core(core_ref, body):
    @pl.when(core_ref[0] == 0)
    def _():
        body(0)

    @pl.when(core_ref[0] == 1)
    def _():
        body(1)


SEEN = ((0, 1, 2), (1, 2, 3))


def in_blocks(core, at, halo_same, halo_cross, mine, theirs):
    block = (halo_same.shape[0] - DOC_ROWS) // 2
    rows = 2 * block

    def parts(x, first=0):
        return (
            x[first : first + block, :],
            x[first + block : first + 2 * block, :],
            x[first + 2 * block : first + 2 * block + DOC_ROWS, :],
        )

    blocks = [mine.at[at], theirs.at[at]]
    kv = [parts(halo_same), parts(halo_cross)] + [parts(x, 2 * rows) for x in blocks]
    queries, upstream = [[x.at[pl.ds(n * rows, rows)] for x in blocks] for n in range(2)]
    if core:
        kv = [kv[1], kv[0], kv[3], kv[2]]
        queries, upstream = queries[::-1], upstream[::-1]
    return kv, queries, upstream


def attend_kernel(at, core_ref, after, *refs):
    inputs, outputs, (doc_cols, probs) = refs[:4], refs[4:8], refs[8:]
    back_same, back_cross, own_out, swap_out = outputs
    size = back_same.shape[1]
    rows = probs.shape[4]
    block = probs.shape[3]
    tile = 256
    scale = size**-0.5

    def column(n):
        return jnp.concatenate([doc_cols[n], doc_cols[n]], axis=1)

    def body(core):
        kv, queries, upstream = in_blocks(core, at, *inputs)
        keys = [x[0] for x in kv]
        values = [x[1] for x in kv]
        for n in range(4):
            line = kv[n][2][:1, :].astype(jnp.float32)
            doc_cols[n] = jnp.broadcast_to(line, (128, block)).T
        key_at = lax.broadcasted_iota(jnp.int32, (block, tile), 0)
        lane = lax.broadcasted_iota(jnp.int32, (block, tile), 1)
        for b in range(2):
            old, full, own = SEEN[b]
            for u in range(rows // tile):
                span = slice(u * tile, (u + 1) * tile)
                q, g = queries[b][span, :], upstream[b][span, :]
                token = lane // 2 + u * (tile // 2)
                doubling = (key_at == token).astype(jnp.bfloat16)
                doc_q = times(kv[2 + b][2], doubling)[:1]
                mine = key_at <= token
                allowed_tri = jnp.where(mine, column(own), column(old)) == doc_q
                allowed_full = column(full) == doc_q
                score_tri = jnp.where(
                    mine, times_transposed(keys[own], q), times_transposed(keys[old], q)
                )
                score_full = times_transposed(keys[full], q)
                tanh_tri = jnp.tanh(score_tri * (scale / SOFTCAP))
                tanh_full = jnp.tanh(score_full * (scale / SOFTCAP))
                exp_tri = jnp.where(allowed_tri, jnp.exp(tanh_tri * SOFTCAP), 0.0)
                exp_full = jnp.where(allowed_full, jnp.exp(tanh_full * SOFTCAP), 0.0)
                total = jnp.sum(exp_tri, axis=0, keepdims=True) + jnp.sum(
                    exp_full, axis=0, keepdims=True
                )
                inverse = 1.0 / total
                prob_tri = exp_tri * inverse
                prob_full = exp_full * inverse
                gp_tri = jnp.where(
                    mine, times_transposed(values[own], g), times_transposed(values[old], g)
                )
                gp_full = times_transposed(values[full], g)
                delta = jnp.sum(prob_tri * gp_tri, axis=0, keepdims=True) + jnp.sum(
                    prob_full * gp_full, axis=0, keepdims=True
                )
                gs_tri = prob_tri * (gp_tri - delta) * (1.0 - tanh_tri * tanh_tri)
                gs_full = prob_full * (gp_full - delta) * (1.0 - tanh_full * tanh_full)
                for n, (tri, full_part) in enumerate(((gs_tri, gs_full), (prob_tri, prob_full))):
                    probs[b, 0, n, :, span] = jnp.where(mine, 0.0, tri).astype(jnp.bfloat16)
                    probs[b, 1, n, :, span] = full_part.astype(jnp.bfloat16)
                    probs[b, 2, n, :, span] = jnp.where(mine, tri, 0.0).astype(jnp.bfloat16)
        backs = (back_same, back_cross) if core == 0 else (back_cross, back_same)
        outs = (own_out, swap_out) if core == 0 else (swap_out, own_out)
        for n, (sides, factor) in enumerate(((queries, scale), (upstream, 1.0))):
            first, second = sides[0][...], sides[1][...]
            sums = (
                times(probs[0, 0, n], first),
                times(probs[0, 1, n], first) + times(probs[1, 0, n], second),
                times(probs[0, 2, n], first) + times(probs[1, 1, n], second),
                times(probs[1, 2, n], second),
            )
            targets = [x.at[pl.ds(n * block, block)] for x in backs]
            targets += [x.at[pl.ds(2 * rows + n * block, block)] for x in outs]
            for total, target in zip(sums, targets):
                target[...] = (total * factor).astype(jnp.bfloat16)
        turned = [(keys[n].T, values[n].T) for n in range(4)]
        for b in range(2):
            for n, factor in enumerate((scale, 1.0)):
                total = sum(times(turned[k][n], probs[b, m, n]) for m, k in enumerate(SEEN[b]))
                first = (1 - n) * rows
                outs[b][first : first + rows, :] = (total.T * factor).astype(jnp.bfloat16)

    by_core(core_ref, body)


def attend(at, core, after, halo_same, halo_cross, mine, theirs):
    block = (halo_same.shape[0] - DOC_ROWS) // 2
    size = halo_same.shape[1]
    rows = 2 * block
    back = jax.ShapeDtypeStruct((2 * block, size), jnp.bfloat16)
    out = jax.ShapeDtypeStruct((2 * rows + 2 * block, size), jnp.bfloat16)
    return pl.pallas_call(
        functools.partial(attend_kernel, at),
        out_shape=(back, back, out, out),
        in_specs=[SMEM, SMEM] + [VMEM] * 4,
        out_specs=(VMEM,) * 4,
        scratch_shapes=[
            pltpu.VMEM((4, block, 128), jnp.float32),
            pltpu.VMEM((2, 3, 2, block, rows), jnp.bfloat16),
        ],
        compiler_params=pltpu.CompilerParams(vmem_limit_bytes=16 << 20),
        cost_estimate=CHEAP,
    )(core, after, halo_same, halo_cross, mine, theirs)


def move(value, pairs):
    return lax.ppermute(value, AXES, pairs)


def local(devices, queries, key_heads, value_heads, grad_output, documents):
    block, heads, size = queries.shape
    kv_heads = key_heads.shape[1]
    chunks = kv_heads // 2
    pair = heads // kv_heads
    forth = [(d, d + 2) for d in range(devices - 2)]
    forth_cross = [(d, (d + 2) ^ 1) for d in range(devices - 2)]
    backward = [(d, s) for s, d in forth]
    backward_cross = [(d, s) for s, d in forth_cross]
    swap = [(d, d ^ 1) for d in range(devices)]

    core = lax.axis_index("inner") % 2
    core_word = core.astype(jnp.int32).reshape(1)
    rows = block * pair

    parts = split(core_word, key_heads, value_heads, documents.reshape(1, block))
    kv_mine, kv_theirs = parts[:chunks], parts[chunks:]
    halo_same, halo_cross = [], []
    for i in range(chunks):
        halo_same.append(move(kv_mine[i], forth))
        halo_cross.append(move(kv_theirs[i], forth_cross))
    mine, theirs = arrange(core_word, queries, grad_output, parts)
    theirs = move(theirs, swap)
    own, swapped, got_same, got_cross = [], [], [], []
    for i in range(chunks):
        after = hold(core_word, halo_same[i], halo_cross[i])
        back_same, back_cross, own_out, swap_out = attend(
            i, core_word, after, halo_same[i], halo_cross[i], mine, theirs
        )
        got_same.append(move(back_same, backward))
        got_cross.append(move(back_cross, backward_cross))
        swapped.append(move(swap_out, swap))
        own.append(own_out)

    after = hold(core_word, got_same[0], got_cross[0], swapped[0])
    attended, grad_queries, placed = spread(core_word, after, block, own, swapped)
    grad_keys, grad_values = gather(
        core_word, block, own, swapped, got_same, got_cross, placed
    )
    return attended, grad_queries, grad_keys, grad_values


def solution(mesh):
    wide = P(AXES, None, None)
    devices = mesh.shape["outer"] * mesh.shape["inner"]
    return jax.shard_map(
        functools.partial(local, devices),
        mesh=mesh,
        in_specs=(wide, wide, wide, wide, P(AXES)),
        out_specs=(wide, wide, wide, wide),
        check_vma=False,
    )
```

```python
import functools

import jax
import jax.numpy as jnp
from jax import lax
from jax.experimental import pallas as pl
from jax.experimental.pallas import tpu as pltpu
from jax.sharding import PartitionSpec as P

SOFTCAP = 50.0
AXES = ("outer", "inner")
VMEM = pl.BlockSpec(memory_space=pltpu.VMEM)
SMEM = pl.BlockSpec(memory_space=pltpu.SMEM)
HBM = pl.BlockSpec(memory_space=pltpu.HBM)
PIECES = 4
HOLD = (40, 10, 100)
DOC_ROWS = 16
CHEAP = pl.CostEstimate(flops=1000, bytes_accessed=1000, transcendentals=0)


def times_transposed(a, b):
    return lax.dot_general(a, b, (((1,), (1,)), ((), ())), preferred_element_type=jnp.float32)


def times(a, b):
    return jnp.dot(a, b, preferred_element_type=jnp.float32)


def pieces(block):
    step = block // PIECES
    return [slice(n * step, (n + 1) * step) for n in range(PIECES)]


def giga_flops(count):
    return pl.CostEstimate(flops=count * 10**9, bytes_accessed=1000, transcendentals=0)


def in_hbm(x):
    return pltpu.with_memory_space_constraint(x, pltpu.HBM)


def fetch(sources, targets, sems):
    copies = []
    for n, at in enumerate(pieces(sources[0].shape[0])):
        for m, (source, target) in enumerate(zip(sources, targets)):
            span = pl.ds(at.start, at.stop - at.start)
            copies.append(pltpu.make_async_copy(source.at[span], target.at[span], sems.at[n, m]))
    for copy in copies:
        copy.start()
    return copies


def split_kernel(core_ref, keys, values, documents, *rest):
    outs, (key_buf, value_buf, doc_buf, sems) = rest[:4], rest[4:]
    block = keys.shape[0]
    copies = fetch((keys, values), (key_buf, value_buf), sems)
    doc_copy = pltpu.make_async_copy(documents, doc_buf, sems.at[PIECES, 0])
    doc_copy.start()

    def place(core):
        for p, at in enumerate(pieces(block)):
            for n, x in enumerate((key_buf, value_buf)):
                copies[2 * p + n].wait()
                for r, out in enumerate(outs):
                    head = (2 * core + r) % 4
                    out[n * block + at.start : n * block + at.stop, :] = x[at, head, :]

    by_core(core_ref, place)

    doc_copy.wait()
    line = (doc_buf[...] + 1).astype(jnp.float32)
    ids = jnp.broadcast_to(line, (DOC_ROWS, block)).astype(jnp.bfloat16)
    for out in outs:
        out[2 * block :, :] = ids


def split(core, keys, values, documents):
    block, heads, size = keys.shape
    shape = jax.ShapeDtypeStruct((2 * block + DOC_ROWS, size), jnp.bfloat16)
    return pl.pallas_call(
        split_kernel,
        out_shape=(shape,) * heads,
        in_specs=[SMEM, HBM, HBM, HBM],
        out_specs=(VMEM,) * heads,
        scratch_shapes=[
            pltpu.VMEM(keys.shape, jnp.bfloat16),
            pltpu.VMEM(values.shape, jnp.bfloat16),
            pltpu.VMEM(documents.shape, jnp.int32),
            pltpu.SemaphoreType.DMA((PIECES + 1, 2)),
        ],
        compiler_params=pltpu.CompilerParams(vmem_limit_bytes=20 << 20),
        cost_estimate=CHEAP,
    )(core, in_hbm(keys), in_hbm(values), in_hbm(documents))


def arrange_kernel(core_ref, queries, upstream, *refs):
    kv, (mine, theirs_0, theirs_1), (query_buf, upstream_buf, sems) = refs[:4], refs[4:7], refs[7:]
    outs = (mine.at[0], mine.at[1], theirs_0, theirs_1)
    block, _, size = queries.shape
    rows = 2 * block
    copies = fetch((queries, upstream), (query_buf, upstream_buf), sems)
    for out, source in zip(outs, kv):
        out[out.shape[0] - source.shape[0] :, :] = source[...]

    def place(core):
        for p, at in enumerate(pieces(block)):
            for n, x in enumerate((query_buf, upstream_buf)):
                copies[2 * p + n].wait()
                for r, out in enumerate(outs):
                    head = (2 * core + r) % 4
                    part = x[at, 2 * head : 2 * head + 2, :].reshape(rows // PIECES, size)
                    out[n * rows + 2 * at.start : n * rows + 2 * at.stop, :] = part

    by_core(core_ref, place)


def arrange(core, queries, upstream, kv):
    block, heads, size = queries.shape
    height = 4 * block + kv[0].shape[0]
    theirs = jax.ShapeDtypeStruct((height, size), jnp.bfloat16)
    return pl.pallas_call(
        arrange_kernel,
        out_shape=(
            jax.ShapeDtypeStruct((2, height, size), jnp.bfloat16),
            theirs,
            theirs,
        ),
        in_specs=[SMEM, HBM, HBM] + [VMEM] * 4,
        out_specs=(VMEM,) * 3,
        scratch_shapes=[
            pltpu.VMEM(queries.shape, jnp.bfloat16),
            pltpu.VMEM(upstream.shape, jnp.bfloat16),
            pltpu.SemaphoreType.DMA((PIECES, 2)),
        ],
        compiler_params=pltpu.CompilerParams(vmem_limit_bytes=20 << 20),
        cost_estimate=CHEAP,
    )(core, in_hbm(queries), in_hbm(upstream), *kv)


def hold_kernel(core_ref, *refs):
    refs[-1][0] = core_ref[0]


def hold(core, giga, *values):
    return pl.pallas_call(
        hold_kernel,
        out_shape=jax.ShapeDtypeStruct((1,), jnp.int32),
        in_specs=[SMEM] + [VMEM] * len(values),
        out_specs=SMEM,
        compiler_params=pltpu.CompilerParams(vmem_limit_bytes=8 << 20),
        cost_estimate=giga_flops(giga),
    )(core, *values)


def spread_kernel(core_ref, after, own_0, own_1, other_0, other_1, *refs):
    outs, done, bufs, sems = refs[:2], refs[2], refs[3:5], refs[5]
    block, _, size = outs[0].shape
    rows = 2 * block
    done[0] = core_ref[0]

    def copies(p, at):
        span = pl.ds(at.start, at.stop - at.start)
        return [
            pltpu.make_async_copy(buf.at[span], out.at[span], sems.at[p, n])
            for n, (buf, out) in enumerate(zip(bufs, outs))
        ]

    def place(core):
        order = (own_0, own_1, other_0, other_1) if core == 0 else (other_0, other_1, own_0, own_1)
        for p, at in enumerate(pieces(block)):
            for n, copy in enumerate(copies(p, at)):
                for g, part in enumerate(order):
                    span = slice(n * rows + 2 * at.start, n * rows + 2 * at.stop)
                    bufs[n][at, 2 * g : 2 * g + 2, :] = part[span, :].reshape(-1, 2, size)
                copy.start()

    by_core(core_ref, place)
    for p, at in enumerate(pieces(block)):
        for copy in copies(p, at):
            copy.wait()


def spread(core, after, block, own, other):
    size = own[0].shape[1]
    shape = jax.ShapeDtypeStruct((block, 8, size), jnp.bfloat16)
    return pl.pallas_call(
        spread_kernel,
        out_shape=(shape, shape, jax.ShapeDtypeStruct((1,), jnp.int32)),
        in_specs=[SMEM, SMEM] + [VMEM] * 4,
        out_specs=(HBM, HBM, SMEM),
        scratch_shapes=[
            pltpu.VMEM((block, 8, size), jnp.bfloat16),
            pltpu.VMEM((block, 8, size), jnp.bfloat16),
            pltpu.SemaphoreType.DMA((PIECES, 2)),
        ],
        compiler_params=pltpu.CompilerParams(vmem_limit_bytes=20 << 20),
        cost_estimate=CHEAP,
    )(core, after, *own, *other)


def gather_kernel(core_ref, *refs):
    own, other, same, cross = refs[:2], refs[2:4], refs[4:6], refs[6:8]
    outs, bufs, sems, wide = refs[9:11], refs[11:13], refs[13], refs[14]
    block = outs[0].shape[0]
    base = own[0].shape[0] - 2 * block
    near, far = list(zip(own, same)), list(zip(other, cross))

    def place(order):
        for p, at in enumerate(pieces(block)):
            for n in range(2):
                for g, (here, there) in enumerate(order):
                    first = n * block + at.start
                    last = n * block + at.stop
                    a = here[base + first : base + last, :].astype(jnp.float32)
                    b = there[first:last, :].astype(jnp.float32)
                    wide[at, g, :] = a + b
                bufs[n][at] = wide[at].astype(jnp.bfloat16)
                span = pl.ds(at.start, at.stop - at.start)
                pltpu.make_async_copy(bufs[n].at[span], outs[n].at[span], sems.at[p, n]).start()

    @pl.when(core_ref[0] == 0)
    def _():
        place(near + far)

    @pl.when(core_ref[0] == 1)
    def _():
        place(far + near)

    for p, at in enumerate(pieces(block)):
        span = pl.ds(at.start, at.stop - at.start)
        for n in range(2):
            pltpu.make_async_copy(bufs[n].at[span], outs[n].at[span], sems.at[p, n]).wait()


def gather(core, block, own, other, same, cross, after):
    size = own[0].shape[1]
    shape = jax.ShapeDtypeStruct((block, 4, size), jnp.bfloat16)
    return pl.pallas_call(
        gather_kernel,
        out_shape=(shape, shape),
        in_specs=[SMEM] + [VMEM] * 8 + [SMEM],
        out_specs=(HBM, HBM),
        scratch_shapes=[
            pltpu.VMEM((block, 4, size), jnp.bfloat16),
            pltpu.VMEM((block, 4, size), jnp.bfloat16),
            pltpu.SemaphoreType.DMA((PIECES, 2)),
            pltpu.VMEM((block, 4, size), jnp.float32),
        ],
        compiler_params=pltpu.CompilerParams(vmem_limit_bytes=20 << 20),
        cost_estimate=CHEAP,
    )(core, *own, *other, *same, *cross, after)


def by_core(core_ref, body):
    @pl.when(core_ref[0] == 0)
    def _():
        body(0)

    @pl.when(core_ref[0] == 1)
    def _():
        body(1)


SEEN = ((0, 1, 2), (1, 2, 3))


def in_blocks(core, at, halo_same, halo_cross, mine, theirs):
    block = (halo_same.shape[0] - DOC_ROWS) // 2
    rows = 2 * block

    def parts(x, first=0):
        return (
            x[first : first + block, :],
            x[first + block : first + 2 * block, :],
            x[first + 2 * block : first + 2 * block + DOC_ROWS, :],
        )

    blocks = [mine.at[at], theirs]
    kv = [parts(halo_same), parts(halo_cross)] + [parts(x, 2 * rows) for x in blocks]
    queries, upstream = [[x.at[pl.ds(n * rows, rows)] for x in blocks] for n in range(2)]
    if core:
        kv = [kv[1], kv[0], kv[3], kv[2]]
        queries, upstream = queries[::-1], upstream[::-1]
    return kv, queries, upstream


def score_kernel(at, core_ref, after, *refs):
    inputs, (back_same, back_cross, parts_out), doc_cols = refs[:4], refs[4:7], refs[7]
    size = back_same.shape[1]
    block = back_same.shape[0] // 2
    rows = 2 * block
    tile = 256
    scale = size**-0.5

    def column(n):
        return jnp.concatenate([doc_cols[n], doc_cols[n]], axis=1)

    def body(core):
        kv, queries, upstream = in_blocks(core, at, *inputs)
        keys = [x[0] for x in kv]
        values = [x[1] for x in kv]
        for n in range(4):
            line = kv[n][2][:1, :].astype(jnp.float32)
            doc_cols[n] = jnp.broadcast_to(line, (128, block)).T
        key_at = lax.broadcasted_iota(jnp.int32, (block, tile), 0)
        lane = lax.broadcasted_iota(jnp.int32, (block, tile), 1)
        sums = [[0.0, 0.0], [0.0, 0.0]]
        for b in range(2):
            old, full, own = SEEN[b]
            for u in range(rows // tile):
                span = slice(u * tile, (u + 1) * tile)
                q, g = queries[b][span, :], upstream[b][span, :]
                token = lane // 2 + u * (tile // 2)
                doubling = (key_at == token).astype(jnp.bfloat16)
                doc_q = times(kv[2 + b][2], doubling)[:1]
                mask = key_at <= token
                allowed_tri = jnp.where(mask, column(own), column(old)) == doc_q
                allowed_full = column(full) == doc_q
                score_tri = jnp.where(
                    mask, times_transposed(keys[own], q), times_transposed(keys[old], q)
                )
                score_full = times_transposed(keys[full], q)
                tanh_tri = jnp.tanh(score_tri * (scale / SOFTCAP))
                tanh_full = jnp.tanh(score_full * (scale / SOFTCAP))
                exp_tri = jnp.where(allowed_tri, jnp.exp(tanh_tri * SOFTCAP), 0.0)
                exp_full = jnp.where(allowed_full, jnp.exp(tanh_full * SOFTCAP), 0.0)
                total = jnp.sum(exp_tri, axis=0, keepdims=True) + jnp.sum(
                    exp_full, axis=0, keepdims=True
                )
                inverse = 1.0 / total
                prob_tri = exp_tri * inverse
                prob_full = exp_full * inverse
                gp_tri = jnp.where(
                    mask, times_transposed(values[own], g), times_transposed(values[old], g)
                )
                gp_full = times_transposed(values[full], g)
                delta = jnp.sum(prob_tri * gp_tri, axis=0, keepdims=True) + jnp.sum(
                    prob_full * gp_full, axis=0, keepdims=True
                )
                gs_tri = prob_tri * (gp_tri - delta) * (1.0 - tanh_tri * tanh_tri)
                gs_full = prob_full * (gp_full - delta) * (1.0 - tanh_full * tanh_full)
                for n, (tri, full_part) in enumerate(((gs_tri, gs_full), (prob_tri, prob_full))):
                    parts = (
                        jnp.where(mask, 0.0, tri).astype(jnp.bfloat16),
                        full_part.astype(jnp.bfloat16),
                        jnp.where(mask, tri, 0.0).astype(jnp.bfloat16),
                    )
                    for m, part in enumerate(parts):
                        parts_out[b, m, n, :, span] = part
                        if b + m < 2:
                            sums[b + m][n] += times(part, (q, g)[n])
        backs = (back_same, back_cross) if core == 0 else (back_cross, back_same)
        for back, (key_sum, value_sum) in zip(backs, sums):
            back[:block, :] = (key_sum * scale).astype(jnp.bfloat16)
            back[block:, :] = value_sum.astype(jnp.bfloat16)

    by_core(core_ref, body)


def score(at, core, after, halo_same, halo_cross, mine, theirs):
    block = (halo_same.shape[0] - DOC_ROWS) // 2
    size = halo_same.shape[1]
    back = jax.ShapeDtypeStruct((2 * block, size), jnp.bfloat16)
    parts = jax.ShapeDtypeStruct((2, 3, 2, block, 2 * block), jnp.bfloat16)
    return pl.pallas_call(
        functools.partial(score_kernel, at),
        out_shape=(back, back, parts),
        in_specs=[SMEM, SMEM] + [VMEM] * 4,
        out_specs=(VMEM,) * 3,
        scratch_shapes=[pltpu.VMEM((4, block, 128), jnp.float32)],
        compiler_params=pltpu.CompilerParams(vmem_limit_bytes=16 << 20),
        cost_estimate=giga_flops(HOLD[1]) if at else CHEAP,
    )(core, after, halo_same, halo_cross, mine, theirs)


def apply_kernel(at, core_ref, *refs):
    inputs, parts, (own_out, swap_out) = refs[:4], refs[4], refs[5:]
    block, rows = parts.shape[3:]
    scale = own_out.shape[1] ** -0.5

    def body(core):
        kv, queries, upstream = in_blocks(core, at, *inputs)
        outs = (own_out, swap_out) if core == 0 else (swap_out, own_out)
        for n, (sides, factor) in enumerate(((queries, scale), (upstream, 1.0))):
            first, second = sides[0][...], sides[1][...]
            sums = (
                times(parts[0, 2, n], first) + times(parts[1, 1, n], second),
                times(parts[1, 2, n], second),
            )
            span = slice(2 * rows + n * block, 2 * rows + (n + 1) * block)
            for total, out in zip(sums, outs):
                out[span, :] = (total * factor).astype(jnp.bfloat16)
            turned = [x[n].T for x in kv]
            for b, out in enumerate(outs):
                total = sum(times(turned[k], parts[b, m, n]) for m, k in enumerate(SEEN[b]))
                at_row = (1 - n) * rows
                out[at_row : at_row + rows, :] = (total * factor).T.astype(jnp.bfloat16)

    by_core(core_ref, body)


def apply(at, core, halo_same, halo_cross, mine, theirs, parts):
    block, rows = parts.shape[3:]
    out = jax.ShapeDtypeStruct((2 * rows + 2 * block, halo_same.shape[1]), jnp.bfloat16)
    return pl.pallas_call(
        functools.partial(apply_kernel, at),
        out_shape=(out, out),
        in_specs=[SMEM] + [VMEM] * 5,
        out_specs=(VMEM,) * 2,
        compiler_params=pltpu.CompilerParams(vmem_limit_bytes=16 << 20),
        cost_estimate=CHEAP,
    )(core, halo_same, halo_cross, mine, theirs, parts)


def move(value, pairs):
    return lax.ppermute(value, AXES, pairs)


def local(devices, queries, key_heads, value_heads, grad_output, documents):
    block, heads, size = queries.shape
    kv_heads = key_heads.shape[1]
    chunks = kv_heads // 2
    pair = heads // kv_heads
    forth = [(d, d + 2) for d in range(devices - 2)]
    forth_cross = [(d, (d + 2) ^ 1) for d in range(devices - 2)]
    backward = [(d, s) for s, d in forth]
    backward_cross = [(d, s) for s, d in forth_cross]
    swap = [(d, d ^ 1) for d in range(devices)]

    core = lax.axis_index("inner") % 2
    core_word = core.astype(jnp.int32).reshape(1)
    rows = block * pair

    parts = split(core_word, key_heads, value_heads, documents.reshape(1, block))
    kv_mine, kv_theirs = parts[:chunks], parts[chunks:]
    halo_same, halo_cross = [], []
    for i in range(chunks):
        halo_same.append(move(kv_mine[i], forth))
        halo_cross.append(move(kv_theirs[i], forth_cross))
    mine, *theirs = arrange(core_word, queries, grad_output, parts)
    theirs = [move(x, swap) for x in theirs]

    got_same, got_cross, parts = [], [], []
    for i in range(chunks):
        if i == 0:
            after = hold(core_word, HOLD[0], halo_same[0], halo_cross[0])
        back_same, back_cross, part = score(
            i, core_word, after, halo_same[i], halo_cross[i], mine, theirs[i]
        )
        got_same.append(move(back_same, backward))
        got_cross.append(move(back_cross, backward_cross))
        parts.append(part)

    own, swapped = [], []
    for i in range(chunks):
        own_out, swap_out = apply(
            i, core_word, halo_same[i], halo_cross[i], mine, theirs[i], parts[i]
        )
        swapped.append(move(swap_out, swap))
        own.append(own_out)

    after = hold(core_word, HOLD[2], got_same[0], got_cross[0])
    attended, grad_queries, placed = spread(core_word, after, block, own, swapped)
    grad_keys, grad_values = gather(
        core_word, block, own, swapped, got_same, got_cross, placed
    )
    return attended, grad_queries, grad_keys, grad_values


def solution(mesh):
    wide = P(AXES, None, None)
    devices = mesh.shape["outer"] * mesh.shape["inner"]
    return jax.shard_map(
        functools.partial(local, devices),
        mesh=mesh,
        in_specs=(wide, wide, wide, wide, P(AXES)),
        out_specs=(wide, wide, wide, wide),
        check_vma=False,
    )
```

```python
import functools

import jax
import jax.numpy as jnp
from jax import lax
from jax.experimental import pallas as pl
from jax.experimental.pallas import tpu as pltpu
from jax.sharding import PartitionSpec as P

SOFTCAP = 50.0
LOG2E = 1.4426950408889634
AXES = ("outer", "inner")
VMEM = pl.BlockSpec(memory_space=pltpu.VMEM)
SMEM = pl.BlockSpec(memory_space=pltpu.SMEM)
HBM = pl.BlockSpec(memory_space=pltpu.HBM)
PIECES = 4
HOLD = (40, 10, 100)
DOC_ROWS = 16
CHEAP = pl.CostEstimate(flops=1000, bytes_accessed=1000, transcendentals=0)


def times_transposed(a, b):
    return lax.dot_general(a, b, (((1,), (1,)), ((), ())), preferred_element_type=jnp.float32)


def times(a, b):
    return jnp.dot(a, b, preferred_element_type=jnp.float32)


def pieces(block):
    step = block // PIECES
    return [slice(n * step, (n + 1) * step) for n in range(PIECES)]


def giga_flops(count):
    return pl.CostEstimate(flops=count * 10**9, bytes_accessed=1000, transcendentals=0)


def in_hbm(x):
    return pltpu.with_memory_space_constraint(x, pltpu.HBM)


def fetch(sources, targets, sems):
    copies = []
    for n, at in enumerate(pieces(sources[0].shape[0])):
        for m, (source, target) in enumerate(zip(sources, targets)):
            span = pl.ds(at.start, at.stop - at.start)
            copies.append(pltpu.make_async_copy(source.at[span], target.at[span], sems.at[n, m]))
    for copy in copies:
        copy.start()
    return copies


def split_kernel(core_ref, keys, values, documents, *rest):
    outs, (key_buf, value_buf, doc_buf, sems) = rest[:4], rest[4:]
    block = keys.shape[0]
    copies = fetch((keys, values), (key_buf, value_buf), sems)
    doc_copy = pltpu.make_async_copy(documents, doc_buf, sems.at[PIECES, 0])
    doc_copy.start()

    def place(core):
        for p, at in enumerate(pieces(block)):
            for n, x in enumerate((key_buf, value_buf)):
                copies[2 * p + n].wait()
                for r, out in enumerate(outs):
                    head = (2 * core + r) % 4
                    out[n * block + at.start : n * block + at.stop, :] = x[at, head, :]

    by_core(core_ref, place)

    doc_copy.wait()
    line = (doc_buf[...] + 1).astype(jnp.float32)
    ids = jnp.broadcast_to(line, (DOC_ROWS, block)).astype(jnp.bfloat16)
    for out in outs:
        out[2 * block :, :] = ids


def split(core, keys, values, documents):
    block, heads, size = keys.shape
    shape = jax.ShapeDtypeStruct((2 * block + DOC_ROWS, size), jnp.bfloat16)
    return pl.pallas_call(
        split_kernel,
        out_shape=(shape,) * heads,
        in_specs=[SMEM, HBM, HBM, HBM],
        out_specs=(VMEM,) * heads,
        scratch_shapes=[
            pltpu.VMEM(keys.shape, jnp.bfloat16),
            pltpu.VMEM(values.shape, jnp.bfloat16),
            pltpu.VMEM(documents.shape, jnp.int32),
            pltpu.SemaphoreType.DMA((PIECES + 1, 2)),
        ],
        compiler_params=pltpu.CompilerParams(vmem_limit_bytes=20 << 20),
        cost_estimate=CHEAP,
    )(core, in_hbm(keys), in_hbm(values), in_hbm(documents))


def arrange_kernel(core_ref, queries, upstream, *refs):
    kv, (mine, theirs), (query_buf, upstream_buf, sems) = refs[:4], refs[4:6], refs[6:]
    outs = (mine.at[0], mine.at[1], theirs.at[0], theirs.at[1])
    block, _, size = queries.shape
    rows = 2 * block
    copies = fetch((queries, upstream), (query_buf, upstream_buf), sems)
    for out, source in zip(outs, kv):
        out[out.shape[0] - source.shape[0] :, :] = source[...]

    def place(core):
        for p, at in enumerate(pieces(block)):
            for n, x in enumerate((query_buf, upstream_buf)):
                copies[2 * p + n].wait()
                for r, out in enumerate(outs):
                    head = (2 * core + r) % 4
                    part = x[at, 2 * head : 2 * head + 2, :].reshape(rows // PIECES, size)
                    out[n * rows + 2 * at.start : n * rows + 2 * at.stop, :] = part

    by_core(core_ref, place)


def arrange(core, queries, upstream, kv):
    block, heads, size = queries.shape
    shape = jax.ShapeDtypeStruct((2, 4 * block + kv[0].shape[0], size), jnp.bfloat16)
    return pl.pallas_call(
        arrange_kernel,
        out_shape=(shape, shape),
        in_specs=[SMEM, HBM, HBM] + [VMEM] * 4,
        out_specs=(VMEM,) * 2,
        scratch_shapes=[
            pltpu.VMEM(queries.shape, jnp.bfloat16),
            pltpu.VMEM(upstream.shape, jnp.bfloat16),
            pltpu.SemaphoreType.DMA((PIECES, 2)),
        ],
        compiler_params=pltpu.CompilerParams(vmem_limit_bytes=20 << 20),
        cost_estimate=CHEAP,
    )(core, in_hbm(queries), in_hbm(upstream), *kv)


def hold_kernel(core_ref, *refs):
    refs[-1][0] = core_ref[0]


def hold(core, giga, *values):
    return pl.pallas_call(
        hold_kernel,
        out_shape=jax.ShapeDtypeStruct((1,), jnp.int32),
        in_specs=[SMEM] + [VMEM] * len(values),
        out_specs=SMEM,
        compiler_params=pltpu.CompilerParams(vmem_limit_bytes=8 << 20),
        cost_estimate=giga_flops(giga),
    )(core, *values)


def spread_kernel(core_ref, after, own_0, own_1, other_0, other_1, *refs):
    outs, done, bufs, sems = refs[:2], refs[2], refs[3:5], refs[5]
    block, _, size = outs[0].shape
    rows = 2 * block
    done[0] = core_ref[0]

    def copies(p, at):
        span = pl.ds(at.start, at.stop - at.start)
        return [
            pltpu.make_async_copy(buf.at[span], out.at[span], sems.at[p, n])
            for n, (buf, out) in enumerate(zip(bufs, outs))
        ]

    def place(core):
        order = (own_0, own_1, other_0, other_1) if core == 0 else (other_0, other_1, own_0, own_1)
        for p, at in enumerate(pieces(block)):
            for n, copy in enumerate(copies(p, at)):
                for g, part in enumerate(order):
                    span = slice(n * rows + 2 * at.start, n * rows + 2 * at.stop)
                    bufs[n][at, 2 * g : 2 * g + 2, :] = part[span, :].reshape(-1, 2, size)
                copy.start()

    by_core(core_ref, place)
    for p, at in enumerate(pieces(block)):
        for copy in copies(p, at):
            copy.wait()


def spread(core, after, block, own, other):
    size = own[0].shape[1]
    shape = jax.ShapeDtypeStruct((block, 8, size), jnp.bfloat16)
    return pl.pallas_call(
        spread_kernel,
        out_shape=(shape, shape, jax.ShapeDtypeStruct((1,), jnp.int32)),
        in_specs=[SMEM, SMEM] + [VMEM] * 4,
        out_specs=(HBM, HBM, SMEM),
        scratch_shapes=[
            pltpu.VMEM((block, 8, size), jnp.bfloat16),
            pltpu.VMEM((block, 8, size), jnp.bfloat16),
            pltpu.SemaphoreType.DMA((PIECES, 2)),
        ],
        compiler_params=pltpu.CompilerParams(vmem_limit_bytes=20 << 20),
        cost_estimate=CHEAP,
    )(core, after, *own, *other)


def gather_kernel(core_ref, *refs):
    own, other, same, cross = refs[:2], refs[2:4], refs[4:6], refs[6:8]
    outs, bufs, sems, wide = refs[9:11], refs[11:13], refs[13], refs[14]
    block = outs[0].shape[0]
    base = own[0].shape[0] - 2 * block
    near, far = list(zip(own, same)), list(zip(other, cross))

    def place(order):
        for p, at in enumerate(pieces(block)):
            for n in range(2):
                for g, (here, there) in enumerate(order):
                    first = n * block + at.start
                    last = n * block + at.stop
                    a = here[base + first : base + last, :].astype(jnp.float32)
                    b = there[first:last, :].astype(jnp.float32)
                    wide[at, g, :] = a + b
                bufs[n][at] = wide[at].astype(jnp.bfloat16)
                span = pl.ds(at.start, at.stop - at.start)
                pltpu.make_async_copy(bufs[n].at[span], outs[n].at[span], sems.at[p, n]).start()

    @pl.when(core_ref[0] == 0)
    def _():
        place(near + far)

    @pl.when(core_ref[0] == 1)
    def _():
        place(far + near)

    for p, at in enumerate(pieces(block)):
        span = pl.ds(at.start, at.stop - at.start)
        for n in range(2):
            pltpu.make_async_copy(bufs[n].at[span], outs[n].at[span], sems.at[p, n]).wait()


def gather(core, block, own, other, same, cross, after):
    size = own[0].shape[1]
    shape = jax.ShapeDtypeStruct((block, 4, size), jnp.bfloat16)
    return pl.pallas_call(
        gather_kernel,
        out_shape=(shape, shape),
        in_specs=[SMEM] + [VMEM] * 8 + [SMEM],
        out_specs=(HBM, HBM),
        scratch_shapes=[
            pltpu.VMEM((block, 4, size), jnp.bfloat16),
            pltpu.VMEM((block, 4, size), jnp.bfloat16),
            pltpu.SemaphoreType.DMA((PIECES, 2)),
            pltpu.VMEM((block, 4, size), jnp.float32),
        ],
        compiler_params=pltpu.CompilerParams(vmem_limit_bytes=20 << 20),
        cost_estimate=CHEAP,
    )(core, *own, *other, *same, *cross, after)


def by_core(core_ref, body):
    @pl.when(core_ref[0] == 0)
    def _():
        body(0)

    @pl.when(core_ref[0] == 1)
    def _():
        body(1)


SEEN = ((0, 1, 2), (1, 2, 3))


def in_blocks(core, at, halo_same, halo_cross, mine, theirs):
    block = (halo_same.shape[0] - DOC_ROWS) // 2
    rows = 2 * block

    def parts(x, first=0):
        return (
            x[first : first + block, :],
            x[first + block : first + 2 * block, :],
            x[first + 2 * block : first + 2 * block + DOC_ROWS, :],
        )

    blocks = [mine.at[at], theirs.at[at]]
    kv = [parts(halo_same), parts(halo_cross)] + [parts(x, 2 * rows) for x in blocks]
    queries, upstream = [[x.at[pl.ds(n * rows, rows)] for x in blocks] for n in range(2)]
    if core:
        kv = [kv[1], kv[0], kv[3], kv[2]]
        queries, upstream = queries[::-1], upstream[::-1]
    return kv, queries, upstream


def score_kernel(at, core_ref, after, *refs):
    inputs, (back_same, back_cross, parts_out), doc_cols = refs[:4], refs[4:7], refs[7]
    size = back_same.shape[1]
    block = back_same.shape[0] // 2
    rows = 2 * block
    tile = 512
    scale = size**-0.5

    def column(n):
        return jnp.concatenate([doc_cols[n]] * (tile // 128), axis=1)

    def body(core):
        kv, queries, upstream = in_blocks(core, at, *inputs)
        keys = [x[0] for x in kv]
        values = [x[1] for x in kv]
        for n in range(4):
            line = kv[n][2][:1, :].astype(jnp.float32)
            doc_cols[n] = jnp.broadcast_to(line, (128, block)).T
        key_at = lax.broadcasted_iota(jnp.int32, (block, tile), 0)
        lane = lax.broadcasted_iota(jnp.int32, (block, tile), 1)
        sums = [[0.0, 0.0], [0.0, 0.0]]
        for b in range(2):
            old, full, own = SEEN[b]
            for u in range(rows // tile):
                span = slice(u * tile, (u + 1) * tile)
                q, g = queries[b][span, :], upstream[b][span, :]
                token = lane // 2 + u * (tile // 2)
                doubling = (key_at == token).astype(jnp.bfloat16)
                doc_q = times(kv[2 + b][2], doubling)[:1]
                mask = key_at <= token
                mask_half = mask.astype(jnp.bfloat16)
                allowed_tri = jnp.where(mask, column(own), column(old)) == doc_q
                allowed_full = column(full) == doc_q
                score_tri = jnp.where(
                    mask, times_transposed(keys[own], q), times_transposed(keys[old], q)
                )
                score_full = times_transposed(keys[full], q)
                tanh_tri = jnp.tanh(score_tri * (scale / SOFTCAP))
                tanh_full = jnp.tanh(score_full * (scale / SOFTCAP))
                exp_tri = jnp.where(allowed_tri, jnp.exp2(tanh_tri * (SOFTCAP * LOG2E)), 0.0)
                exp_full = jnp.where(allowed_full, jnp.exp2(tanh_full * (SOFTCAP * LOG2E)), 0.0)
                total = jnp.sum(exp_tri, axis=0, keepdims=True) + jnp.sum(
                    exp_full, axis=0, keepdims=True
                )
                inverse = 1.0 / total
                prob_tri = exp_tri * inverse
                prob_full = exp_full * inverse
                gp_tri = jnp.where(
                    mask, times_transposed(values[own], g), times_transposed(values[old], g)
                )
                gp_full = times_transposed(values[full], g)
                delta = jnp.sum(prob_tri * gp_tri, axis=0, keepdims=True) + jnp.sum(
                    prob_full * gp_full, axis=0, keepdims=True
                )
                gs_tri = prob_tri * (gp_tri - delta) * (1.0 - tanh_tri * tanh_tri)
                gs_full = prob_full * (gp_full - delta) * (1.0 - tanh_full * tanh_full)
                for n, (tri, full_part) in enumerate(((gs_tri, gs_full), (prob_tri, prob_full))):
                    tri = tri.astype(jnp.bfloat16)
                    own_part = tri * mask_half
                    parts = (tri - own_part, full_part.astype(jnp.bfloat16), own_part)
                    for m, part in enumerate(parts):
                        parts_out[b, m, n, :, span] = part
                        if b + m < 2:
                            sums[b + m][n] += times(part, (q, g)[n])
        backs = (back_same, back_cross) if core == 0 else (back_cross, back_same)
        for back, (key_sum, value_sum) in zip(backs, sums):
            back[:block, :] = (key_sum * scale).astype(jnp.bfloat16)
            back[block:, :] = value_sum.astype(jnp.bfloat16)

    by_core(core_ref, body)


def score(at, core, after, halo_same, halo_cross, mine, theirs):
    block = (halo_same.shape[0] - DOC_ROWS) // 2
    size = halo_same.shape[1]
    back = jax.ShapeDtypeStruct((2 * block, size), jnp.bfloat16)
    parts = jax.ShapeDtypeStruct((2, 3, 2, block, 2 * block), jnp.bfloat16)
    return pl.pallas_call(
        functools.partial(score_kernel, at),
        out_shape=(back, back, parts),
        in_specs=[SMEM, SMEM] + [VMEM] * 4,
        out_specs=(VMEM,) * 3,
        scratch_shapes=[pltpu.VMEM((4, block, 128), jnp.float32)],
        compiler_params=pltpu.CompilerParams(vmem_limit_bytes=16 << 20),
        cost_estimate=giga_flops(HOLD[1]) if at else CHEAP,
    )(core, after, halo_same, halo_cross, mine, theirs)


def apply_kernel(at, core_ref, *refs):
    inputs, parts, (own_out, swap_out) = refs[:4], refs[4], refs[5:]
    block, rows = parts.shape[3:]
    scale = own_out.shape[1] ** -0.5

    def body(core):
        kv, queries, upstream = in_blocks(core, at, *inputs)
        outs = (own_out, swap_out) if core == 0 else (swap_out, own_out)
        for n, (sides, factor) in enumerate(((queries, scale), (upstream, 1.0))):
            first, second = sides[0][...], sides[1][...]
            sums = (
                times(parts[0, 2, n], first) + times(parts[1, 1, n], second),
                times(parts[1, 2, n], second),
            )
            span = slice(2 * rows + n * block, 2 * rows + (n + 1) * block)
            for total, out in zip(sums, outs):
                out[span, :] = (total * factor).astype(jnp.bfloat16)
            turned = [x[n].T for x in kv]
            for b, out in enumerate(outs):
                total = sum(times(turned[k], parts[b, m, n]) for m, k in enumerate(SEEN[b]))
                at_row = (1 - n) * rows
                out[at_row : at_row + rows, :] = (total * factor).T.astype(jnp.bfloat16)

    by_core(core_ref, body)


def apply(at, core, halo_same, halo_cross, mine, theirs, parts):
    block, rows = parts.shape[3:]
    out = jax.ShapeDtypeStruct((2 * rows + 2 * block, halo_same.shape[1]), jnp.bfloat16)
    return pl.pallas_call(
        functools.partial(apply_kernel, at),
        out_shape=(out, out),
        in_specs=[SMEM] + [VMEM] * 5,
        out_specs=(VMEM,) * 2,
        compiler_params=pltpu.CompilerParams(vmem_limit_bytes=16 << 20),
        cost_estimate=CHEAP,
    )(core, halo_same, halo_cross, mine, theirs, parts)


def move(value, pairs):
    return lax.ppermute(value, AXES, pairs)


def local(devices, queries, key_heads, value_heads, grad_output, documents):
    block, heads, size = queries.shape
    kv_heads = key_heads.shape[1]
    chunks = kv_heads // 2
    pair = heads // kv_heads
    forth = [(d, d + 2) for d in range(devices - 2)]
    forth_cross = [(d, (d + 2) ^ 1) for d in range(devices - 2)]
    backward = [(d, s) for s, d in forth]
    backward_cross = [(d, s) for s, d in forth_cross]
    swap = [(d, d ^ 1) for d in range(devices)]

    core = lax.axis_index("inner") % 2
    core_word = core.astype(jnp.int32).reshape(1)
    rows = block * pair

    parts = split(core_word, key_heads, value_heads, documents.reshape(1, block))
    kv_mine, kv_theirs = parts[:chunks], parts[chunks:]
    halo_same, halo_cross = [], []
    for i in range(chunks):
        halo_same.append(move(kv_mine[i], forth))
        halo_cross.append(move(kv_theirs[i], forth_cross))
    mine, theirs = arrange(core_word, queries, grad_output, parts)
    theirs = move(theirs, swap)

    got_same, got_cross, parts = [], [], []
    for i in range(chunks):
        if i == 0:
            after = hold(core_word, HOLD[0], halo_same[0], halo_cross[0])
        back_same, back_cross, part = score(
            i, core_word, after, halo_same[i], halo_cross[i], mine, theirs
        )
        got_same.append(move(back_same, backward))
        got_cross.append(move(back_cross, backward_cross))
        parts.append(part)

    own, swapped = [], []
    for i in range(chunks):
        own_out, swap_out = apply(
            i, core_word, halo_same[i], halo_cross[i], mine, theirs, parts[i]
        )
        swapped.append(move(swap_out, swap))
        own.append(own_out)

    after = hold(core_word, HOLD[2], got_same[0], got_cross[0])
    attended, grad_queries, placed = spread(core_word, after, block, own, swapped)
    grad_keys, grad_values = gather(
        core_word, block, own, swapped, got_same, got_cross, placed
    )
    return attended, grad_queries, grad_keys, grad_values


def solution(mesh):
    wide = P(AXES, None, None)
    devices = mesh.shape["outer"] * mesh.shape["inner"]
    return jax.shard_map(
        functools.partial(local, devices),
        mesh=mesh,
        in_specs=(wide, wide, wide, wide, P(AXES)),
        out_specs=(wide, wide, wide, wide),
        check_vma=False,
    )
```

```python
import functools

import jax
import jax.numpy as jnp
from jax import lax
from jax.experimental import pallas as pl
from jax.experimental.pallas import tpu as pltpu
from jax.sharding import PartitionSpec as P

SOFTCAP = 50.0
LOG2E = 1.4426950408889634
AXES = ("outer", "inner")
VMEM = pl.BlockSpec(memory_space=pltpu.VMEM)
SMEM = pl.BlockSpec(memory_space=pltpu.SMEM)
HBM = pl.BlockSpec(memory_space=pltpu.HBM)
PIECES = 4
HOLD = (40, 10, 100)
DOC_ROWS = 16
CHEAP = pl.CostEstimate(flops=1000, bytes_accessed=1000, transcendentals=0)


def times_transposed(a, b):
    return lax.dot_general(a, b, (((1,), (1,)), ((), ())), preferred_element_type=jnp.float32)


def times(a, b):
    return jnp.dot(a, b, preferred_element_type=jnp.float32)


def pieces(block):
    step = block // PIECES
    return [slice(n * step, (n + 1) * step) for n in range(PIECES)]


def giga_flops(count):
    return pl.CostEstimate(flops=count * 10**9, bytes_accessed=1000, transcendentals=0)


def in_hbm(x):
    return pltpu.with_memory_space_constraint(x, pltpu.HBM)


def fetch(sources, targets, sems):
    copies = []
    for n, at in enumerate(pieces(sources[0].shape[0])):
        for m, (source, target) in enumerate(zip(sources, targets)):
            span = pl.ds(at.start, at.stop - at.start)
            copies.append(pltpu.make_async_copy(source.at[span], target.at[span], sems.at[n, m]))
    for copy in copies:
        copy.start()
    return copies


def split_kernel(core_ref, keys, values, documents, *rest):
    outs, (key_buf, value_buf, doc_buf, sems) = rest[:4], rest[4:]
    block = keys.shape[0]
    copies = fetch((keys, values), (key_buf, value_buf), sems)
    doc_copy = pltpu.make_async_copy(documents, doc_buf, sems.at[PIECES, 0])
    doc_copy.start()

    def place(core):
        for p, at in enumerate(pieces(block)):
            for n, x in enumerate((key_buf, value_buf)):
                copies[2 * p + n].wait()
                for r, out in enumerate(outs):
                    head = (2 * core + r) % 4
                    out[n * block + at.start : n * block + at.stop, :] = x[at, head, :]

    by_core(core_ref, place)

    doc_copy.wait()
    line = (doc_buf[...] + 1).astype(jnp.float32)
    ids = jnp.broadcast_to(line, (DOC_ROWS, block)).astype(jnp.bfloat16)
    for out in outs:
        out[2 * block :, :] = ids


def split(core, keys, values, documents):
    block, heads, size = keys.shape
    shape = jax.ShapeDtypeStruct((2 * block + DOC_ROWS, size), jnp.bfloat16)
    return pl.pallas_call(
        split_kernel,
        out_shape=(shape,) * heads,
        in_specs=[SMEM, HBM, HBM, HBM],
        out_specs=(VMEM,) * heads,
        scratch_shapes=[
            pltpu.VMEM(keys.shape, jnp.bfloat16),
            pltpu.VMEM(values.shape, jnp.bfloat16),
            pltpu.VMEM(documents.shape, jnp.int32),
            pltpu.SemaphoreType.DMA((PIECES + 1, 2)),
        ],
        compiler_params=pltpu.CompilerParams(vmem_limit_bytes=20 << 20),
        cost_estimate=CHEAP,
    )(core, in_hbm(keys), in_hbm(values), in_hbm(documents))


def arrange_kernel(core_ref, queries, upstream, *refs):
    kv, (mine, theirs), (query_buf, upstream_buf, sems) = refs[:4], refs[4:6], refs[6:]
    outs = (mine.at[0], mine.at[1], theirs.at[0], theirs.at[1])
    block, _, size = queries.shape
    rows = 2 * block
    copies = fetch((queries, upstream), (query_buf, upstream_buf), sems)
    for out, source in zip(outs, kv):
        out[out.shape[0] - source.shape[0] :, :] = source[...]

    def place(core):
        for p, at in enumerate(pieces(block)):
            for n, x in enumerate((query_buf, upstream_buf)):
                copies[2 * p + n].wait()
                for r, out in enumerate(outs):
                    head = (2 * core + r) % 4
                    part = x[at, 2 * head : 2 * head + 2, :].reshape(rows // PIECES, size)
                    out[n * rows + 2 * at.start : n * rows + 2 * at.stop, :] = part

    by_core(core_ref, place)


def arrange(core, queries, upstream, kv):
    block, heads, size = queries.shape
    shape = jax.ShapeDtypeStruct((2, 4 * block + kv[0].shape[0], size), jnp.bfloat16)
    return pl.pallas_call(
        arrange_kernel,
        out_shape=(shape, shape),
        in_specs=[SMEM, HBM, HBM] + [VMEM] * 4,
        out_specs=(VMEM,) * 2,
        scratch_shapes=[
            pltpu.VMEM(queries.shape, jnp.bfloat16),
            pltpu.VMEM(upstream.shape, jnp.bfloat16),
            pltpu.SemaphoreType.DMA((PIECES, 2)),
        ],
        compiler_params=pltpu.CompilerParams(vmem_limit_bytes=20 << 20),
        cost_estimate=CHEAP,
    )(core, in_hbm(queries), in_hbm(upstream), *kv)


def hold_kernel(core_ref, *refs):
    refs[-1][0] = core_ref[0]


def hold(core, giga, *values):
    return pl.pallas_call(
        hold_kernel,
        out_shape=jax.ShapeDtypeStruct((1,), jnp.int32),
        in_specs=[SMEM] + [VMEM] * len(values),
        out_specs=SMEM,
        compiler_params=pltpu.CompilerParams(vmem_limit_bytes=8 << 20),
        cost_estimate=giga_flops(giga),
    )(core, *values)


def spread_kernel(core_ref, after, own_0, own_1, other_0, other_1, *refs):
    outs, done, bufs, sems = refs[:2], refs[2], refs[3:5], refs[5]
    block, _, size = outs[0].shape
    rows = 2 * block
    done[0] = core_ref[0]

    def copies(p, at):
        span = pl.ds(at.start, at.stop - at.start)
        return [
            pltpu.make_async_copy(buf.at[span], out.at[span], sems.at[p, n])
            for n, (buf, out) in enumerate(zip(bufs, outs))
        ]

    def place(core):
        order = (own_0, own_1, other_0, other_1) if core == 0 else (other_0, other_1, own_0, own_1)
        for p, at in enumerate(pieces(block)):
            for n, copy in enumerate(copies(p, at)):
                for g, part in enumerate(order):
                    span = slice(n * rows + 2 * at.start, n * rows + 2 * at.stop)
                    bufs[n][at, 2 * g : 2 * g + 2, :] = part[span, :].reshape(-1, 2, size)
                copy.start()

    by_core(core_ref, place)
    for p, at in enumerate(pieces(block)):
        for copy in copies(p, at):
            copy.wait()


def spread(core, after, block, own, other):
    size = own[0].shape[1]
    shape = jax.ShapeDtypeStruct((block, 8, size), jnp.bfloat16)
    return pl.pallas_call(
        spread_kernel,
        out_shape=(shape, shape, jax.ShapeDtypeStruct((1,), jnp.int32)),
        in_specs=[SMEM, SMEM] + [VMEM] * 4,
        out_specs=(HBM, HBM, SMEM),
        scratch_shapes=[
            pltpu.VMEM((block, 8, size), jnp.bfloat16),
            pltpu.VMEM((block, 8, size), jnp.bfloat16),
            pltpu.SemaphoreType.DMA((PIECES, 2)),
        ],
        compiler_params=pltpu.CompilerParams(vmem_limit_bytes=20 << 20),
        cost_estimate=CHEAP,
    )(core, after, *own, *other)


def add_heads(core, wide, at, chunk, own, other, same, cross):
    block = wide.shape[1]
    base = own.shape[0] - 2 * block
    for r, here, there in ((chunk, own, same), (2 + chunk, other, cross)):
        for n in range(2):
            first, last = n * block + at.start, n * block + at.stop
            a = here[base + first : base + last, :].astype(jnp.float32)
            b = there[first:last, :].astype(jnp.float32)
            wide[n, at, (2 * core + r) % 4, :] = a + b


def begin_kernel(core_ref, own, other, same, cross, after, wide):
    by_core(
        core_ref,
        lambda core: add_heads(core, wide, slice(0, wide.shape[1]), 0, own, other, same, cross),
    )


def begin(core, block, own, other, same, cross, after):
    return pl.pallas_call(
        begin_kernel,
        out_shape=jax.ShapeDtypeStruct((2, block, 4, own.shape[1]), jnp.float32),
        in_specs=[SMEM] + [VMEM] * 4 + [SMEM],
        out_specs=VMEM,
        compiler_params=pltpu.CompilerParams(vmem_limit_bytes=20 << 20),
        cost_estimate=CHEAP,
    )(core, own, other, same, cross, after)


def gather_kernel(core_ref, own, other, same, cross, started, *refs):
    outs, wide, bufs, sems = refs[:2], refs[2], refs[3:5], refs[5]
    block = wide.shape[1]

    def copies(p, at):
        span = pl.ds(at.start, at.stop - at.start)
        return [
            pltpu.make_async_copy(buf.at[span], out.at[span], sems.at[p, n])
            for n, (buf, out) in enumerate(zip(bufs, outs))
        ]

    def place(core):
        for p, at in enumerate(pieces(block)):
            add_heads(core, wide, at, 1, own, other, same, cross)
            for n, copy in enumerate(copies(p, at)):
                bufs[n][at] = wide[n, at].astype(jnp.bfloat16)
                copy.start()

    by_core(core_ref, place)
    for p, at in enumerate(pieces(block)):
        for copy in copies(p, at):
            copy.wait()


def gather(core, block, own, other, same, cross, started):
    size = own.shape[1]
    shape = jax.ShapeDtypeStruct((block, 4, size), jnp.bfloat16)
    return pl.pallas_call(
        gather_kernel,
        out_shape=(shape, shape, jax.ShapeDtypeStruct(started.shape, jnp.float32)),
        in_specs=[SMEM] + [VMEM] * 5,
        out_specs=(HBM, HBM, VMEM),
        input_output_aliases={5: 2},
        scratch_shapes=[
            pltpu.VMEM((block, 4, size), jnp.bfloat16),
            pltpu.VMEM((block, 4, size), jnp.bfloat16),
            pltpu.SemaphoreType.DMA((PIECES, 2)),
        ],
        compiler_params=pltpu.CompilerParams(vmem_limit_bytes=20 << 20),
        cost_estimate=CHEAP,
    )(core, own, other, same, cross, started)[:2]


def by_core(core_ref, body):
    @pl.when(core_ref[0] == 0)
    def _():
        body(0)

    @pl.when(core_ref[0] == 1)
    def _():
        body(1)


SEEN = ((0, 1, 2), (1, 2, 3))


def in_blocks(core, at, halo_same, halo_cross, mine, theirs):
    block = (halo_same.shape[0] - DOC_ROWS) // 2
    rows = 2 * block

    def parts(x, first=0):
        return (
            x[first : first + block, :],
            x[first + block : first + 2 * block, :],
            x[first + 2 * block : first + 2 * block + DOC_ROWS, :],
        )

    blocks = [mine.at[at], theirs.at[at]]
    kv = [parts(halo_same), parts(halo_cross)] + [parts(x, 2 * rows) for x in blocks]
    queries, upstream = [[x.at[pl.ds(n * rows, rows)] for x in blocks] for n in range(2)]
    if core:
        kv = [kv[1], kv[0], kv[3], kv[2]]
        queries, upstream = queries[::-1], upstream[::-1]
    return kv, queries, upstream


def score_kernel(at, core_ref, after, *refs):
    inputs, (back_same, back_cross, parts_out), doc_cols = refs[:4], refs[4:7], refs[7]
    size = back_same.shape[1]
    block = back_same.shape[0] // 2
    rows = 2 * block
    tile = 512
    scale = size**-0.5

    def column(n):
        return jnp.concatenate([doc_cols[n]] * (tile // 128), axis=1)

    def body(core):
        kv, queries, upstream = in_blocks(core, at, *inputs)
        keys = [x[0] for x in kv]
        values = [x[1] for x in kv]
        for n in range(4):
            line = kv[n][2][:1, :].astype(jnp.float32)
            doc_cols[n] = jnp.broadcast_to(line, (128, block)).T
        key_at = lax.broadcasted_iota(jnp.int32, (block, tile), 0)
        lane = lax.broadcasted_iota(jnp.int32, (block, tile), 1)
        sums = [[0.0, 0.0], [0.0, 0.0]]
        for b in range(2):
            old, full, own = SEEN[b]
            for u in range(rows // tile):
                span = slice(u * tile, (u + 1) * tile)
                q, g = queries[b][span, :], upstream[b][span, :]
                token = lane // 2 + u * (tile // 2)
                doubling = (key_at == token).astype(jnp.bfloat16)
                doc_q = times(kv[2 + b][2], doubling)[:1]
                mask = key_at <= token
                mask_half = mask.astype(jnp.bfloat16)
                allowed_tri = jnp.where(mask, column(own), column(old)) == doc_q
                allowed_full = column(full) == doc_q
                score_tri = jnp.where(
                    mask, times_transposed(keys[own], q), times_transposed(keys[old], q)
                )
                score_full = times_transposed(keys[full], q)
                tanh_tri = jnp.tanh(score_tri * (scale / SOFTCAP))
                tanh_full = jnp.tanh(score_full * (scale / SOFTCAP))
                exp_tri = jnp.where(allowed_tri, jnp.exp2(tanh_tri * (SOFTCAP * LOG2E)), 0.0)
                exp_full = jnp.where(allowed_full, jnp.exp2(tanh_full * (SOFTCAP * LOG2E)), 0.0)
                total = jnp.sum(exp_tri, axis=0, keepdims=True) + jnp.sum(
                    exp_full, axis=0, keepdims=True
                )
                inverse = 1.0 / total
                prob_tri = exp_tri * inverse
                prob_full = exp_full * inverse
                gp_tri = jnp.where(
                    mask, times_transposed(values[own], g), times_transposed(values[old], g)
                )
                gp_full = times_transposed(values[full], g)
                delta = jnp.sum(prob_tri * gp_tri, axis=0, keepdims=True) + jnp.sum(
                    prob_full * gp_full, axis=0, keepdims=True
                )
                gs_tri = prob_tri * (gp_tri - delta) * (1.0 - tanh_tri * tanh_tri)
                gs_full = prob_full * (gp_full - delta) * (1.0 - tanh_full * tanh_full)
                for n, (tri, full_part) in enumerate(((gs_tri, gs_full), (prob_tri, prob_full))):
                    tri = tri.astype(jnp.bfloat16)
                    own_part = tri * mask_half
                    parts = (tri - own_part, full_part.astype(jnp.bfloat16), own_part)
                    for m, part in enumerate(parts):
                        parts_out[b, m, n, :, span] = part
                        if b + m < 2:
                            sums[b + m][n] += times(part, (q, g)[n])
        backs = (back_same, back_cross) if core == 0 else (back_cross, back_same)
        for back, (key_sum, value_sum) in zip(backs, sums):
            back[:block, :] = (key_sum * scale).astype(jnp.bfloat16)
            back[block:, :] = value_sum.astype(jnp.bfloat16)

    by_core(core_ref, body)


def score(at, core, after, halo_same, halo_cross, mine, theirs):
    block = (halo_same.shape[0] - DOC_ROWS) // 2
    size = halo_same.shape[1]
    back = jax.ShapeDtypeStruct((2 * block, size), jnp.bfloat16)
    parts = jax.ShapeDtypeStruct((2, 3, 2, block, 2 * block), jnp.bfloat16)
    return pl.pallas_call(
        functools.partial(score_kernel, at),
        out_shape=(back, back, parts),
        in_specs=[SMEM, SMEM] + [VMEM] * 4,
        out_specs=(VMEM,) * 3,
        scratch_shapes=[pltpu.VMEM((4, block, 128), jnp.float32)],
        compiler_params=pltpu.CompilerParams(vmem_limit_bytes=16 << 20),
        cost_estimate=giga_flops(HOLD[1]) if at else CHEAP,
    )(core, after, halo_same, halo_cross, mine, theirs)


def apply_kernel(at, core_ref, *refs):
    inputs, parts, (own_out, swap_out) = refs[:4], refs[4], refs[5:]
    block, rows = parts.shape[3:]
    scale = own_out.shape[1] ** -0.5

    def body(core):
        kv, queries, upstream = in_blocks(core, at, *inputs)
        outs = (own_out, swap_out) if core == 0 else (swap_out, own_out)
        for n, (sides, factor) in enumerate(((queries, scale), (upstream, 1.0))):
            first, second = sides[0][...], sides[1][...]
            sums = (
                times(parts[0, 2, n], first) + times(parts[1, 1, n], second),
                times(parts[1, 2, n], second),
            )
            span = slice(2 * rows + n * block, 2 * rows + (n + 1) * block)
            for total, out in zip(sums, outs):
                out[span, :] = (total * factor).astype(jnp.bfloat16)
            turned = [x[n].T for x in kv]
            for b, out in enumerate(outs):
                total = sum(times(turned[k], parts[b, m, n]) for m, k in enumerate(SEEN[b]))
                at_row = (1 - n) * rows
                out[at_row : at_row + rows, :] = (total * factor).T.astype(jnp.bfloat16)

    by_core(core_ref, body)


def apply(at, core, halo_same, halo_cross, mine, theirs, parts):
    block, rows = parts.shape[3:]
    out = jax.ShapeDtypeStruct((2 * rows + 2 * block, halo_same.shape[1]), jnp.bfloat16)
    return pl.pallas_call(
        functools.partial(apply_kernel, at),
        out_shape=(out, out),
        in_specs=[SMEM] + [VMEM] * 5,
        out_specs=(VMEM,) * 2,
        compiler_params=pltpu.CompilerParams(vmem_limit_bytes=16 << 20),
        cost_estimate=CHEAP,
    )(core, halo_same, halo_cross, mine, theirs, parts)


def move(value, pairs):
    return lax.ppermute(value, AXES, pairs)


def local(devices, queries, key_heads, value_heads, grad_output, documents):
    block, heads, size = queries.shape
    kv_heads = key_heads.shape[1]
    chunks = kv_heads // 2
    pair = heads // kv_heads
    forth = [(d, d + 2) for d in range(devices - 2)]
    forth_cross = [(d, (d + 2) ^ 1) for d in range(devices - 2)]
    backward = [(d, s) for s, d in forth]
    backward_cross = [(d, s) for s, d in forth_cross]
    swap = [(d, d ^ 1) for d in range(devices)]

    core = lax.axis_index("inner") % 2
    core_word = core.astype(jnp.int32).reshape(1)
    rows = block * pair

    parts = split(core_word, key_heads, value_heads, documents.reshape(1, block))
    kv_mine, kv_theirs = parts[:chunks], parts[chunks:]
    halo_same, halo_cross = [], []
    for i in range(chunks):
        halo_same.append(move(kv_mine[i], forth))
        halo_cross.append(move(kv_theirs[i], forth_cross))
    mine, theirs = arrange(core_word, queries, grad_output, parts)
    theirs = move(theirs, swap)

    got_same, got_cross, parts = [], [], []
    for i in range(chunks):
        if i == 0:
            after = hold(core_word, HOLD[0], halo_same[0], halo_cross[0])
        back_same, back_cross, part = score(
            i, core_word, after, halo_same[i], halo_cross[i], mine, theirs
        )
        got_same.append(move(back_same, backward))
        got_cross.append(move(back_cross, backward_cross))
        parts.append(part)

    own, swapped = [], []
    for i in range(chunks):
        own_out, swap_out = apply(
            i, core_word, halo_same[i], halo_cross[i], mine, theirs, parts[i]
        )
        swapped.append(move(swap_out, swap))
        own.append(own_out)

    after = hold(core_word, HOLD[2], got_same[0], got_cross[0])
    attended, grad_queries, placed = spread(core_word, after, block, own, swapped)
    terms = list(zip(own, swapped, got_same, got_cross))
    started = begin(core_word, block, *terms[0], placed)
    grad_keys, grad_values = gather(core_word, block, *terms[1], started)
    return attended, grad_queries, grad_keys, grad_values


def solution(mesh):
    wide = P(AXES, None, None)
    devices = mesh.shape["outer"] * mesh.shape["inner"]
    return jax.shard_map(
        functools.partial(local, devices),
        mesh=mesh,
        in_specs=(wide, wide, wide, wide, P(AXES)),
        out_specs=(wide, wide, wide, wide),
        check_vma=False,
    )
```
